256 devices in a mesh: aux: 8 (over y_lo, x), occ: 32 (over z, y_hi, core).
Axes of the slice: x: 4, y: 4 (y_hi: 2, y_lo: 2; y = y_hi * 2 + y_lo), z: 8, core: 2. Of those that a mesh axis runs over, the one named last changes fastest.
Arguments:
- orbital_slabs: bfloat16 [256, 64, 24576], P('occ', None, 'aux'), may hold values from -0.5 to 0.5
- occ_energy: bfloat16 [256], P('occ'), may hold values from -1.1953125 to -0.29882812
- virt_energy: bfloat16 [64], replicated, may hold values from 0.29882812 to 2.5
- pair_kept: int32 [32], replicated, may hold values 0 or 1
Outputs:
- gamma: bfloat16 [256, 64, 24576], P('occ', None, 'aux')
- virt_density: float32 [64, 64], replicated
The draws below stay inside these ranges and needn't reach their ends.
All inputs are finite; a program needn't handle non-finite values.
Results may differ from the reference program's by a relative error of at most 0.019.
Values may be sent and summed in bfloat16 or wider, within the bound.
No kernel may reach another device: no remote copies, remote signals or barrier semaphores. Data moves between devices by JAX's collectives and lax.ppermute only.
A program may use at most 64 MiB of HBM per device.

```python
import jax
import jax.numpy as jnp
from jax import lax

OCC_DEV = 8
VB = 64
AUX_DEV = 3072
BLOCKS = 32
NOCC = 256
AUX = 24576
N_AUX = 8
N_OCC = 32


def place_ends(entries, stream_key, smallest, largest):
    longest = entries.shape.index(max(entries.shape))
    spots = []
    for shift in (0, 1):
        where = [jax.random.randint(jax.random.fold_in(stream_key, axis), (), 0, length) for axis, length in enumerate(entries.shape)]
        where[longest] = (where[longest] + shift) % entries.shape[longest]
        spots.append(tuple(where))
    return entries.at[spots[0]].set(smallest).at[spots[1]].set(largest)


def block_levels(own_key, dims, shards, least, top_value):
    factor_of, own = 1.0, jax.random.fold_in(own_key, 6)
    for axis_at, blocks in shards:
        draws = jnp.exp(jax.random.uniform(jax.random.fold_in(own, axis_at), (blocks,), jnp.float32, least / len(shards), top_value / len(shards)))
        factor_of = factor_of * jnp.repeat(draws, dims[axis_at] // blocks).reshape([-1 if axis == axis_at else 1 for axis in range(len(dims))])
    return factor_of


def scatter_about(key, dims, spread, most, pieces=(), kind=jnp.bfloat16):
    drawn = jax.random.normal(key, dims, jnp.float32) * spread
    if len(pieces) > 0:
        drawn = block_levels(key, dims, pieces, -0.22, 0.18) * drawn
    return jnp.clip(drawn, min=-most, max=most).astype(kind)


def setup_inputs(seed: int = 0) -> dict:
    key_list = jax.random.split(jax.random.key(seed), 5)
    orbital_slabs = scatter_about(key_list[0], (NOCC, VB, AUX), 0.08, 0.5, ((0, 32), (2, 8)))
    occ_energy = jnp.clip(-1.1953125 + 0.8964844 * jax.random.uniform(key_list[1], (NOCC,), jnp.float32) ** block_levels(key_list[1], (NOCC,), ((0, 32),), -0.2, 0.2), -1.1953125, -0.29882812).astype(jnp.bfloat16)
    virt_energy = jnp.clip(jax.random.uniform(key_list[2], (VB,), jnp.float32, 0.29882812, 2.5), 0.29882812, 2.5).astype(jnp.bfloat16)
    pair_kept = place_ends((jax.random.randint(key_list[3], (BLOCKS,), 0, 4) < 3).astype(jnp.int32), jax.random.fold_in(key_list[3], 1), 0, 1)
    return dict(orbital_slabs=orbital_slabs, occ_energy=occ_energy, virt_energy=virt_energy, pair_kept=pair_kept)


def pair_amplitudes(left, right, left_energy, right_energy, virt_energy, keep):
    rows = left.shape[0] * left.shape[1]
    grouped_left = left.reshape(rows, N_AUX, AUX_DEV).astype(jnp.float32)
    grouped_right = right.reshape(rows, N_AUX, AUX_DEV).astype(jnp.float32)
    partial_value = jnp.einsum("rgp,sgp->grs", grouped_left, grouped_right).astype(jnp.bfloat16)
    integrals = jnp.sum(partial_value.astype(jnp.float32), axis=0)
    virt_values = virt_energy.astype(jnp.float32)
    gap_left = (left_energy.astype(jnp.float32)[:, None] - virt_values[None, :]).reshape(rows)
    gap_right = (right_energy.astype(jnp.float32)[:, None] - virt_values[None, :]).reshape(rows)
    amplitude = (keep * integrals / (gap_left[:, None] + gap_right[None, :])).astype(jnp.bfloat16)
    wide = amplitude.astype(jnp.float32).reshape(OCC_DEV, VB, OCC_DEV, VB)
    tilde = (2.0 * wide - wide.transpose(0, 3, 2, 1)).astype(jnp.bfloat16)
    return amplitude, tilde.reshape(rows, rows)


def pair_density(amplitude, tilde, both):
    amp_four = amplitude.astype(jnp.float32).reshape(OCC_DEV, VB, OCC_DEV, VB)
    til_four = tilde.astype(jnp.float32).reshape(OCC_DEV, VB, OCC_DEV, VB)
    total = jnp.einsum("iajc,ibjc->ab", til_four, amp_four)
    if both:
        total = total + jnp.einsum("icja,icjb->ab", til_four, amp_four)
    return total


def reference(orbital_slabs, occ_energy, virt_energy, pair_kept):
    rows = OCC_DEV * VB

    def block(index):
        start = (index * OCC_DEV).astype(jnp.int32)
        return (lax.dynamic_slice_in_dim(orbital_slabs, start, OCC_DEV, 0),
                lax.dynamic_slice_in_dim(occ_energy, start, OCC_DEV, 0))

    def step(density, index):
        following = ((index + 1) % N_OCC).astype(jnp.int32)
        preceding = ((index + N_OCC - 1) % N_OCC).astype(jnp.int32)
        slabs, energy = block(index)
        next_slabs, next_energy = block(following)
        prev_slabs, prev_energy = block(preceding)
        keep_next = pair_kept[index].astype(jnp.float32)
        keep_prev = pair_kept[preceding].astype(jnp.float32)
        amp_self, tilde_self = pair_amplitudes(slabs, slabs, energy, energy, virt_energy, jnp.float32(1.0))
        amp_next, tilde_next = pair_amplitudes(slabs, next_slabs, energy, next_energy, virt_energy, keep_next)
        amp_prev, tilde_prev = pair_amplitudes(prev_slabs, slabs, prev_energy, energy, virt_energy, keep_prev)
        flat = slabs.reshape(rows, AUX)
        own = jnp.dot(tilde_self, flat, preferred_element_type=jnp.float32)
        own = own + jnp.dot(tilde_next, next_slabs.reshape(rows, AUX), preferred_element_type=jnp.float32)
        returned = jnp.dot(tilde_prev.T, prev_slabs.reshape(rows, AUX), preferred_element_type=jnp.float32).astype(jnp.bfloat16)
        gamma_block = (own + returned.astype(jnp.float32)).astype(jnp.bfloat16)
        density = density + pair_density(amp_self, tilde_self, False) + pair_density(amp_next, tilde_next, True)
        return density, gamma_block

    density, gammas = lax.scan(step, jnp.zeros((VB, VB), jnp.float32), jnp.arange(N_OCC, dtype=jnp.int32))
    gamma = gammas.reshape(NOCC, VB, AUX)
    return gamma, density / (4.0 * OCC_DEV * OCC_DEV * VB)
```

```python
import functools

import jax
import jax.numpy as jnp
from jax import lax
from jax.experimental import pallas as pl
from jax.experimental.pallas import tpu as pltpu
from jax.sharding import PartitionSpec as P

F32 = jnp.float32
BF16 = jnp.bfloat16
MIB = 1 << 20
X = 4
Q = 128


def params(mib):
    return pltpu.CompilerParams(
        dimension_semantics=("arbitrary",), vmem_limit_bytes=mib * MIB
    )


def rows_product(left, right):
    return lax.dot_general(left, right, (((1,), (1,)), ((), ())), preferred_element_type=F32)


def product(left, right):
    return lax.dot_general(left, right, (((1,), (0,)), ((), ())), preferred_element_type=F32)


def early_integrals_kernel(info, own, other, o0, o1, o2, o3, total_own, total_inner):
    step = pl.program_id(0)

    @pl.when(step == 0)
    def _():
        total_own[...] = jnp.zeros_like(total_own)
        total_inner[...] = jnp.zeros_like(total_inner)

    mine = own[...]
    theirs = other[...]
    total_own[...] += rows_product(mine, mine)

    def half(block, parity):
        return jnp.concatenate(
            [block[(2 * q + parity) * 64 : (2 * q + parity + 1) * 64] for q in range(4)], axis=0
        )

    @pl.when(info[0] == 0)
    def _():
        total_inner[...] += rows_product(half(mine, 0), theirs)

    @pl.when(info[0] == 1)
    def _():
        total_inner[...] += rows_product(half(theirs, 1), mine)

    @pl.when(step == pl.num_programs(0) - 1)
    def _():
        for d, out in enumerate((o0, o1, o2, o3)):
            q = lax.rem(info[1] + d, X)
            out[0:128, :] = total_own[pl.ds(pl.multiple_of(q * 128, 128), 128), :].astype(BF16)
            out[128:192, :] = total_inner[pl.ds(pl.multiple_of(q * 64, 64), 64), :].astype(BF16)


def early_integrals(info, own, other):
    rows, aux = own.shape
    width = 768
    slab = pl.BlockSpec((rows, width), lambda s, info: (0, s))
    piece = pl.BlockSpec((192, rows), lambda s, info: (0, 0))
    return pl.pallas_call(
        early_integrals_kernel,
        grid_spec=pltpu.PrefetchScalarGridSpec(
            num_scalar_prefetch=1,
            grid=(aux // width,),
            in_specs=[slab, slab],
            out_specs=[piece] * 4,
            scratch_shapes=[pltpu.VMEM((rows, rows), F32), pltpu.VMEM((rows // 2, rows), F32)],
        ),
        out_shape=[jax.ShapeDtypeStruct((192, rows), BF16)] * 4,
        compiler_params=params(32),
        cost_estimate=pl.CostEstimate(
            flops=3 * rows * rows * aux, bytes_accessed=4 * rows * aux, transcendentals=0
        ),
        name="early_integrals",
    )(info, own, other)


def late_integrals_kernel(info, own, following, o0, o1, o2, o3, total):
    step = pl.program_id(0)

    @pl.when(info[0] == 1)
    def _():
        @pl.when(step == 0)
        def _():
            total[...] = jnp.zeros_like(total)

        total[...] += rows_product(own[...], following[...])

        @pl.when(step == pl.num_programs(0) - 1)
        def _():
            for d, out in enumerate((o0, o1, o2, o3)):
                q = lax.rem(info[1] + d, X)
                out[...] = total[pl.ds(pl.multiple_of(q * 128, 128), 128), :].astype(BF16)

    @pl.when(jnp.logical_and(info[0] == 0, step == 0))
    def _():
        for out in (o0, o1, o2, o3):
            out[...] = jnp.zeros_like(out)


def late_integrals(info, own, following):
    rows, aux = own.shape
    width = 768
    slab = pl.BlockSpec((rows, width), lambda s, info: (0, s * info[0]))
    piece = pl.BlockSpec((Q, rows), lambda s, info: (0, 0))
    return pl.pallas_call(
        late_integrals_kernel,
        grid_spec=pltpu.PrefetchScalarGridSpec(
            num_scalar_prefetch=1,
            grid=(aux // width,),
            in_specs=[slab, slab],
            out_specs=[piece] * 4,
            scratch_shapes=[pltpu.VMEM((rows, rows), F32)],
        ),
        out_shape=[jax.ShapeDtypeStruct((Q, rows), BF16)] * 4,
        compiler_params=params(32),
        cost_estimate=pl.CostEstimate(
            flops=2 * rows * rows * aux, bytes_accessed=4 * rows * aux, transcendentals=0
        ),
        name="late_integrals",
    )(info, own, following)


def block_transposed(wide):
    turned = wide.T
    top, bottom = turned[:64], turned[64:]
    low = lax.broadcasted_iota(jnp.int32, (64, 128), 1) < 64
    first = jnp.where(low, top, pltpu.roll(bottom, 64, 1))
    second = jnp.where(low, pltpu.roll(top, 64, 1), bottom)
    return jnp.concatenate([first, second], axis=0), turned


def diagonal_blocks(square):
    return square[:64, :64] + pltpu.roll(square[64:, :], 64, 1)[:, :64]


def tilde_rows(integrals, gap_left, gap_right, keep, store):
    first = jnp.zeros((128, 128), F32)
    second = jnp.zeros((128, 128), F32)
    for J in range(4):
        at = slice(J * 128, (J + 1) * 128)
        amp = (keep * integrals(at) / (gap_left + gap_right[:, at])).astype(BF16)
        wide = amp.astype(F32)
        swapped, turned = block_transposed(wide)
        tilde_wide = (2.0 * wide - swapped).astype(BF16).astype(F32)
        tilde = tilde_wide.astype(BF16)
        tilde_turned = tilde_wide.T.astype(BF16)
        first += rows_product(tilde, amp)
        second += rows_product(tilde_turned, turned.astype(BF16))
        store(J, tilde, tilde_turned)
    return diagonal_blocks(first), diagonal_blocks(second)


def early_tilde_kernel(info, keep, sums, inner_other, gl_own, gr_own, gl_in, gr_in, out, density):
    def store_own(J, tilde, turned):
        out[J] = tilde

    own_first, _ = tilde_rows(
        lambda at: sums[0:128, at], gl_own[...], gr_own[...], 1.0, store_own
    )
    left_home = info[0] == 0

    def inner(at):
        mine, theirs = sums[128:192, at], inner_other[:, at]
        return jnp.concatenate(
            [jnp.where(left_home, mine, theirs), jnp.where(left_home, theirs, mine)], axis=0
        )

    def store_inner(J, tilde, turned):
        out[4 + J] = jnp.where(left_home, tilde, turned)

    first, second = tilde_rows(inner, gl_in[...], gr_in[...], keep[0], store_inner)
    density[...] = own_first + jnp.where(left_home, first + second, 0.0)


SMEM = pl.BlockSpec(memory_space=pltpu.SMEM)
VMEM = pl.BlockSpec(memory_space=pltpu.VMEM)


def early_tilde(info, keep, sums, inner_other, *gaps):
    return pl.pallas_call(
        early_tilde_kernel,
        in_specs=[SMEM, SMEM] + [VMEM] * 6,
        out_specs=[VMEM, VMEM],
        out_shape=[jax.ShapeDtypeStruct((8, 128, 128), BF16), jax.ShapeDtypeStruct((64, 64), F32)],
        compiler_params=pltpu.CompilerParams(vmem_limit_bytes=32 * MIB),
        cost_estimate=pl.CostEstimate(flops=1 << 26, bytes_accessed=1 << 20, transcendentals=0),
        name="early_tilde",
    )(info, keep, sums, inner_other, *gaps)


def late_tilde_kernel(info, keep, mine, partner, near, far, early, gl, gr, out, density):
    left_home = info[0] == 1

    def outer(at):
        here = mine[:, at].astype(F32) + partner[:, at].astype(F32)
        there = near[:, at].astype(F32) + far[:, at].astype(F32)
        return jnp.where(left_home, here, there)

    def store(J, tilde, turned):
        out[J] = jnp.where(left_home, tilde, turned)

    first, second = tilde_rows(outer, gl[...], gr[...], keep[1], store)
    density[...] = early[...] + jnp.where(left_home, first + second, 0.0)


def late_tilde(info, keep, *rest):
    return pl.pallas_call(
        late_tilde_kernel,
        in_specs=[SMEM, SMEM] + [VMEM] * 7,
        out_specs=[VMEM, VMEM],
        out_shape=[jax.ShapeDtypeStruct((4, 128, 128), BF16), jax.ShapeDtypeStruct((64, 64), F32)],
        compiler_params=pltpu.CompilerParams(vmem_limit_bytes=32 * MIB),
        cost_estimate=pl.CostEstimate(flops=1 << 25, bytes_accessed=1 << 20, transcendentals=0),
        name="late_tilde",
    )(info, keep, *rest)


def early_gamma_kernel(info, p0, p1, p2, p3, own, other, out, factors):
    @pl.when(pl.program_id(0) == 0)
    def _():
        for d, piece in enumerate((p0, p1, p2, p3)):
            q = lax.rem(info[1] + X - d, X)
            here = pl.ds(pl.multiple_of(q * 128, 128), 128)
            for J in range(4):
                factors[here, J * 128 : (J + 1) * 128] = piece[J]

            @pl.when(info[0] == 0)
            def _():
                for J in range(4):
                    factors[here, 512 + J * 128 : 512 + (J + 1) * 128] = piece[4 + J]

            @pl.when(info[0] == 1)
            def _():
                column = pl.ds(pl.multiple_of(512 + q * 128, 128), 128)
                for J in range(4):
                    factors[J * 128 : (J + 1) * 128, column] = piece[4 + J]

    out[...] = product(factors[:, :512], own[...]) + product(factors[:, 512:], other[...])


def early_gamma(info, pieces, own, other):
    rows, aux = own.shape
    width = 768
    slab = pl.BlockSpec((rows, width), lambda s, info: (0, s))
    piece = pl.BlockSpec((8, 128, 128), lambda s, info: (0, 0, 0))
    return pl.pallas_call(
        early_gamma_kernel,
        grid_spec=pltpu.PrefetchScalarGridSpec(
            num_scalar_prefetch=1,
            grid=(aux // width,),
            in_specs=[piece] * 4 + [slab, slab],
            out_specs=slab,
            scratch_shapes=[pltpu.VMEM((rows, 2 * rows), BF16)],
        ),
        out_shape=jax.ShapeDtypeStruct((rows, aux), F32),
        compiler_params=params(32),
        cost_estimate=pl.CostEstimate(
            flops=4 * rows * rows * aux, bytes_accessed=8 * rows * aux, transcendentals=0
        ),
        name="early_gamma",
    )(info, *pieces, own, other)


def late_gamma_kernel(info, p0, p1, p2, p3, early, following, preceding, out, factors):
    @pl.when(pl.program_id(0) == 0)
    def _():
        for d, piece in enumerate((p0, p1, p2, p3)):
            q = lax.rem(info[1] + X - d, X)
            here = pl.ds(pl.multiple_of(q * 128, 128), 128)

            @pl.when(info[0] == 1)
            def _():
                for J in range(4):
                    factors[here, J * 128 : (J + 1) * 128] = piece[J]

            @pl.when(info[0] == 0)
            def _():
                for J in range(4):
                    factors[J * 128 : (J + 1) * 128, here] = piece[J]

    @pl.when(info[0] == 1)
    def _():
        out[...] = (early[...] + product(factors[...], following[...])).astype(BF16)

    @pl.when(info[0] == 0)
    def _():
        out[...] = (early[...] + product(factors[...], preceding[...])).astype(BF16)


def late_gamma(info, pieces, early, following, preceding):
    rows, aux = early.shape
    width = 768
    slab = pl.BlockSpec((rows, width), lambda s, info: (0, s))
    on_left = pl.BlockSpec((rows, width), lambda s, info: (0, s * info[0]))
    on_right = pl.BlockSpec((rows, width), lambda s, info: (0, s * (1 - info[0])))
    piece = pl.BlockSpec((4, 128, 128), lambda s, info: (0, 0, 0))
    return pl.pallas_call(
        late_gamma_kernel,
        grid_spec=pltpu.PrefetchScalarGridSpec(
            num_scalar_prefetch=1,
            grid=(aux // width,),
            in_specs=[piece] * 4 + [slab, on_left, on_right],
            out_specs=slab,
            scratch_shapes=[pltpu.VMEM((rows, rows), BF16)],
        ),
        out_shape=jax.ShapeDtypeStruct((rows, aux), BF16),
        compiler_params=params(32),
        cost_estimate=pl.CostEstimate(
            flops=2 * rows * rows * aux, bytes_accessed=8 * rows * aux, transcendentals=0
        ),
        name="late_gamma",
    )(info, *pieces, early, following, preceding)


def along_x(value, by):
    return lax.ppermute(
        value, "aux", [(a, a // X * X + (a + by) % X) for a in range(lax.axis_size("aux"))]
    )


def across_y(value):
    count = lax.axis_size("aux")
    return lax.ppermute(value, "aux", [(a, (a + X) % count) for a in range(count)])


def left_homes_to(value, forward, by=0, turn=0):
    aux, occ = lax.axis_size("aux"), lax.axis_size("occ")

    def aux_to(a):
        return (a // X * X + turn * X) % aux + (a + by) % X

    return lax.ppermute(
        value,
        ("aux", "occ"),
        [
            (a * occ + k, aux_to(a) * occ + (k + forward) % occ)
            for a in range(aux)
            for k in range(1, occ, 2)
        ],
    )


def swapped(value, axis, other):
    return lax.ppermute(value, axis, [(k, other(k)) for k in range(lax.axis_size(axis))])


def after(value, *earlier):
    return lax.optimization_barrier((value, *earlier))[0]


def gap(energy, virt_energy):
    return (energy.astype(F32)[:, None] - virt_energy.astype(F32)[None, :]).reshape(-1)


def body(orbital_slabs, occ_energy, virt_energy, pair_kept):
    occ_count, virt_count, aux_count = orbital_slabs.shape
    rows = occ_count * virt_count
    occ = lax.axis_size("occ")
    slabs = orbital_slabs.reshape(rows, aux_count)
    place = lax.axis_index("occ")
    core = lax.rem(place, 2)
    x = lax.rem(lax.axis_index("aux"), X)
    info = jnp.stack([core, x]).astype(jnp.int32)

    def outer_partner(k):
        return (k + 1) % occ if k % 2 else (k - 1) % occ

    following = lax.ppermute(slabs, "occ", [(k, (k - 1) % occ) for k in range(0, occ, 2)])
    other = swapped(slabs, "occ", lambda k: k ^ 1)
    inner_energy = swapped(occ_energy, "occ", lambda k: k ^ 1)
    outer_energy = swapped(occ_energy, "occ", outer_partner)

    own_gap = gap(occ_energy, virt_energy)
    inner_gap = gap(inner_energy, virt_energy)
    outer_gap = gap(outer_energy, virt_energy)
    first_core = core == 0

    def rows_of(values):
        return lax.dynamic_slice_in_dim(values, x * Q, Q, 0).reshape(Q, 1)

    gl_own, gr_own = rows_of(own_gap), own_gap.reshape(1, rows)
    gl_in = rows_of(jnp.where(first_core, own_gap, inner_gap))
    gr_in = jnp.where(first_core, inner_gap, own_gap).reshape(1, rows)
    gl_out = rows_of(jnp.where(first_core, outer_gap, own_gap))
    gr_out = jnp.where(first_core, own_gap, outer_gap).reshape(1, rows)
    keep_in = pair_kept[place - core].astype(F32)
    keep_out = pair_kept[lax.rem(place - 1 + core + occ, occ)].astype(F32)
    keep = jnp.stack([keep_in, keep_out])

    pieces = early_integrals(info, slabs, other)
    arrived = [along_x(pieces[d], d) for d in (1, 2, 3)]
    sums = pieces[0].astype(F32)
    for value in arrived:
        sums = sums + value.astype(F32)
    sums = sums.astype(BF16)
    sums = sums.astype(F32) + across_y(sums).astype(F32)
    inner_other = swapped(sums[Q:], "occ", lambda k: k ^ 1)
    tilde, density = early_tilde(info, keep, sums, inner_other, gl_own, gr_own, gl_in, gr_in)
    gathered = [tilde] + [along_x(tilde, d) for d in (1, 2, 3)]
    early = early_gamma(info, gathered, slabs, other)

    preceding = lax.ppermute(
        after(slabs, following), "occ", [(k, (k + 1) % occ) for k in range(1, occ, 2)]
    )
    pieces = late_integrals(info, slabs, following)
    arrived = [left_homes_to(pieces[d], 0, by=d) for d in (1, 2, 3)]
    sums = pieces[0].astype(F32)
    for value in arrived:
        sums = sums + value.astype(F32)
    sums = sums.astype(BF16)
    partner = left_homes_to(sums, 0, turn=1)
    near = left_homes_to(sums, 1)
    far = left_homes_to(sums, 1, turn=1)
    tilde, density = late_tilde(info, keep, sums, partner, near, far, density, gl_out, gr_out)
    gathered = [tilde] + [along_x(tilde, d) for d in (1, 2, 3)]

    count = lax.axis_size("aux")
    for bit in (1, 2):
        density = density + lax.ppermute(density, "aux", [(a, a ^ bit) for a in range(count)])
    bit = 1
    while bit < occ:
        density = density + swapped(density, "occ", lambda k, bit=bit: k ^ bit)
        bit *= 2
    virt_density = density / (4.0 * occ_count * occ_count * virt_count)

    gamma = late_gamma(info, gathered, early, following, preceding)
    return gamma.reshape(occ_count, virt_count, aux_count), virt_density


def solution(mesh):
    return jax.shard_map(
        body,
        mesh=mesh,
        in_specs=(P("occ", None, "aux"), P("occ"), P(), P()),
        out_specs=(P("occ", None, "aux"), P()),
        check_vma=False,
    )
```

```python
import functools

import jax
import jax.numpy as jnp
from jax import lax
from jax.experimental import pallas as pl
from jax.experimental.pallas import tpu as pltpu
from jax.sharding import PartitionSpec as P

F32 = jnp.float32
BF16 = jnp.bfloat16
MIB = 1 << 20
X = 4
CHUNKS = 4
SMEM = pl.BlockSpec(memory_space=pltpu.SMEM)
VMEM = pl.BlockSpec(memory_space=pltpu.VMEM)
ANY = pl.BlockSpec(memory_space=pl.ANY)
Q = 128


def params(mib):
    return pltpu.CompilerParams(vmem_limit_bytes=mib * MIB)


def rows_product(left, right):
    return lax.dot_general(left, right, (((1,), (1,)), ((), ())), preferred_element_type=F32)


def product(left, right):
    return lax.dot_general(left, right, (((1,), (0,)), ((), ())), preferred_element_type=F32)


def owned(info, x):
    return x ^ info[2]


def owned_late(info, x):
    return x ^ info[2] ^ (2 - 2 * info[0])


KEEP = 24


def chunks(aux):
    width = aux // CHUNKS
    return [slice(c * width, (c + 1) * width) for c in range(CHUNKS)]


def fetched(source, target, semaphores):
    return [
        pltpu.make_async_copy(source.at[:, at], target.at[:, at], semaphores.at[c])
        for c, at in enumerate(chunks(source.shape[1]))
    ]


def early_integrals_kernel(
    info, own, other, o0, o1, o2, o3, mine, theirs, total_own, total_inner, sem_mine, sem_theirs
):
    own_copies = fetched(own, mine, sem_mine)
    other_copies = fetched(other, theirs, sem_theirs)
    for copy in own_copies + other_copies:
        copy.start()

    def add(total, value, first):
        if first:
            total[...] = value
        else:
            total[...] += value

    for c, at in enumerate(chunks(own.shape[1])):
        own_copies[c].wait()
        add(total_own, rows_product(mine[:, at], mine[:, at]), c == 0)

    def half(block, at, parity):
        return jnp.concatenate(
            [block[(2 * q + parity) * 64 : (2 * q + parity + 1) * 64, at] for q in range(4)], axis=0
        )

    for c, at in enumerate(chunks(own.shape[1])):
        other_copies[c].wait()

        @pl.when(info[0] == 0)
        def _():
            add(total_inner, rows_product(half(mine, at, 0), theirs[:, at]), c == 0)

        @pl.when(info[0] == 1)
        def _():
            add(total_inner, rows_product(half(theirs, at, 1), mine[:, at]), c == 0)

    for d, out in enumerate((o0, o1, o2, o3)):
        q = owned(info, lax.rem(info[1] + d, X))
        out[0:128, :] = total_own[pl.ds(pl.multiple_of(q * 128, 128), 128), :].astype(BF16)
        out[128:192, :] = total_inner[pl.ds(pl.multiple_of(q * 64, 64), 64), :].astype(BF16)


def early_integrals(info, own, other):
    rows, aux = own.shape
    return pl.pallas_call(
        early_integrals_kernel,
        in_specs=[SMEM, ANY, ANY],
        out_specs=[VMEM] * 4,
        out_shape=[jax.ShapeDtypeStruct((192, rows), BF16)] * 4,
        scratch_shapes=[
            pltpu.VMEM((rows, aux), BF16),
            pltpu.VMEM((rows, aux), BF16),
            pltpu.VMEM((rows, rows), F32),
            pltpu.VMEM((rows // 2, rows), F32),
            pltpu.SemaphoreType.DMA((CHUNKS,)),
            pltpu.SemaphoreType.DMA((CHUNKS,)),
        ],
        compiler_params=params(40),
        cost_estimate=pl.CostEstimate(flops=0, bytes_accessed=0, transcendentals=0),
        name="early_integrals",
    )(info, own, other)


def late_integrals_kernel(
    info, own, following, o0, o1, o2, o3, mine, theirs, total, sem_mine, sem_theirs
):
    @pl.when(info[0] == 1)
    def _():
        own_copies = fetched(own, mine, sem_mine)
        other_copies = fetched(following, theirs, sem_theirs)
        for pair in zip(own_copies, other_copies):
            for copy in pair:
                copy.start()
        for c, at in enumerate(chunks(own.shape[1])):
            own_copies[c].wait()
            other_copies[c].wait()
            value = rows_product(mine[:, at], theirs[:, at])
            if c == 0:
                total[...] = value
            else:
                total[...] += value
        for d, out in enumerate((o0, o1, o2, o3)):
            q = owned(info, lax.rem(info[1] + d, X))
            out[...] = total[pl.ds(pl.multiple_of(q * 128, 128), 128), :].astype(BF16)

    @pl.when(info[0] == 0)
    def _():
        for out in (o0, o1, o2, o3):
            out[...] = jnp.zeros_like(out)


def late_integrals(info, own, following):
    rows, aux = own.shape
    return pl.pallas_call(
        late_integrals_kernel,
        in_specs=[SMEM, ANY, ANY],
        out_specs=[VMEM] * 4,
        out_shape=[jax.ShapeDtypeStruct((Q, rows), BF16)] * 4,
        scratch_shapes=[
            pltpu.VMEM((rows, aux), BF16),
            pltpu.VMEM((rows, aux), BF16),
            pltpu.VMEM((rows, rows), F32),
            pltpu.SemaphoreType.DMA((CHUNKS,)),
            pltpu.SemaphoreType.DMA((CHUNKS,)),
        ],
        compiler_params=params(40),
        cost_estimate=pl.CostEstimate(flops=0, bytes_accessed=0, transcendentals=0),
        name="late_integrals",
    )(info, own, following)


def block_transposed(wide):
    turned = wide.T
    top, bottom = turned[:64], turned[64:]
    low = lax.broadcasted_iota(jnp.int32, (64, 128), 1) < 64
    first = jnp.where(low, top, pltpu.roll(bottom, 64, 1))
    second = jnp.where(low, pltpu.roll(top, 64, 1), bottom)
    return jnp.concatenate([first, second], axis=0), turned


def diagonal_blocks(square):
    return square[:64, :64] + pltpu.roll(square[64:, :], 64, 1)[:, :64]


def tilde_rows(integrals, q, left, right, along, keep, store):
    first = jnp.zeros((128, 128), F32)
    second = jnp.zeros((128, 128), F32)
    upper = lax.broadcasted_iota(jnp.int32, (128, 1), 0) < 64
    lower = lax.broadcasted_iota(jnp.int32, (1, 128), 1) < 64
    down = jnp.broadcast_to(along, (128, 128)).T
    gap_left = jnp.where(upper, left(2 * q), left(2 * q + 1)) - down
    for J in range(4):
        at = slice(J * 128, (J + 1) * 128)
        gap_right = jnp.where(lower, right(2 * J), right(2 * J + 1)) - along
        amp = (keep * integrals(at) / (gap_left + gap_right)).astype(BF16)
        wide = amp.astype(F32)
        swapped, turned = block_transposed(wide)
        tilde_wide = (2.0 * wide - swapped).astype(BF16).astype(F32)
        tilde = tilde_wide.astype(BF16)
        tilde_turned = tilde_wide.T.astype(BF16)
        first += rows_product(tilde, amp)
        second += rows_product(tilde_turned, turned.astype(BF16))
        store(J, tilde, tilde_turned)
    return diagonal_blocks(first), diagonal_blocks(second)


def early_tilde_kernel(info, table, sums, inner_other, along, out, density):
    q = owned(info, info[1])
    left_home = info[0] == 0

    def own(i):
        return table[i]

    def left(i):
        return table[8 * info[0] + i]

    def right(j):
        return table[8 - 8 * info[0] + j]

    def store_own(J, tilde, turned):
        out[J] = tilde

    own_first, _ = tilde_rows(
        lambda at: sums[0:128, at], q, own, own, along[...], 1.0, store_own
    )

    def inner(at):
        mine, theirs = sums[128:192, at], inner_other[:, at]
        return jnp.concatenate(
            [jnp.where(left_home, mine, theirs), jnp.where(left_home, theirs, mine)], axis=0
        )

    def store_inner(J, tilde, turned):
        out[4 + J] = jnp.where(left_home, tilde, turned)

    first, second = tilde_rows(
        inner, q, left, right, along[...], table[KEEP], store_inner
    )
    density[...] = own_first + jnp.where(left_home, first + second, 0.0)


def early_tilde(info, table, *rest):
    return pl.pallas_call(
        early_tilde_kernel,
        in_specs=[SMEM] * 2 + [VMEM] * 3,
        out_specs=[VMEM, VMEM],
        out_shape=[jax.ShapeDtypeStruct((8, 128, 128), BF16), jax.ShapeDtypeStruct((64, 64), F32)],
        compiler_params=pltpu.CompilerParams(vmem_limit_bytes=32 * MIB),
        cost_estimate=pl.CostEstimate(flops=0, bytes_accessed=0, transcendentals=0),
        name="early_tilde",
    )(info, table, *rest)


def folded(square):
    return jnp.concatenate([square[:32], square[32:]], axis=1)


def late_tilde_kernel(info, table, near, far, partner, mine, early, along, out):
    left_home = info[0] == 1

    def left(i):
        return table[16 - 16 * info[0] + i]

    def right(j):
        return table[16 * info[0] + j]

    def outer(at):
        here = mine[:, at].astype(F32) + partner[:, at].astype(F32)
        there = near[:, at].astype(F32) + far[:, at].astype(F32)
        return jnp.where(left_home, here, there)

    def store(J, tilde, turned):
        out[J * 128 : (J + 1) * 128, :] = jnp.where(left_home, tilde, turned)

    first, second = tilde_rows(
        outer, owned_late(info, info[1]), left, right, along[...], table[KEEP + 1], store
    )
    total = early[...] + jnp.where(left_home, 0.0, first + second)
    high = total.astype(BF16)
    out[512:544, :] = folded(high)
    out[544:576, :] = folded((total - high.astype(F32)).astype(BF16))


def late_tilde(info, table, *rest):
    return pl.pallas_call(
        late_tilde_kernel,
        in_specs=[SMEM] * 2 + [VMEM] * 6,
        out_specs=VMEM,
        out_shape=jax.ShapeDtypeStruct((576, 128), BF16),
        compiler_params=pltpu.CompilerParams(vmem_limit_bytes=32 * MIB),
        cost_estimate=pl.CostEstimate(flops=0, bytes_accessed=0, transcendentals=0),
        name="late_tilde",
    )(info, table, *rest)


def gamma_kernel(
    info, e0, e1, e2, e3, p0, p1, p2, p3, own, other, following, preceding, out,
    slab, result, factors, sem_own, sem_other, sem_outer, sem_out,
):
    rows = own.shape[0]
    left_home = info[0] == 1
    own_copies = fetched(own, slab.at[:rows], sem_own)
    other_copies = fetched(other, slab.at[rows : 2 * rows], sem_other)
    left_copies = fetched(following, slab.at[2 * rows :], sem_outer)
    right_copies = fetched(preceding, slab.at[2 * rows :], sem_outer)
    for c in range(CHUNKS):
        own_copies[c].start()
        other_copies[c].start()

        @pl.when(left_home)
        def _():
            left_copies[c].start()

        @pl.when(jnp.logical_not(left_home))
        def _():
            right_copies[c].start()

    for d, (early, late) in enumerate(((e0, p0), (e1, p1), (e2, p2), (e3, p3))):
        q = owned(info, lax.rem(info[1] + X - d, X))
        here = pl.ds(pl.multiple_of(q * 128, 128), 128)
        for J in range(4):
            factors[here, J * 128 : (J + 1) * 128] = early[J]

        q_late = owned_late(info, lax.rem(info[1] + X - d, X))
        here_late = pl.ds(pl.multiple_of(q_late * 128, 128), 128)

        @pl.when(jnp.logical_not(left_home))
        def _():
            column = pl.ds(pl.multiple_of(2 * rows + q_late * 128, 128), 128)
            for J in range(4):
                factors[here, rows + J * 128 : rows + (J + 1) * 128] = early[4 + J]
                factors[J * 128 : (J + 1) * 128, column] = late[J * 128 : (J + 1) * 128]

        @pl.when(left_home)
        def _():
            column = pl.ds(pl.multiple_of(rows + q * 128, 128), 128)
            for J in range(4):
                factors[J * 128 : (J + 1) * 128, column] = early[4 + J]
                factors[here_late, 2 * rows + J * 128 : 2 * rows + (J + 1) * 128] = late[
                    J * 128 : (J + 1) * 128
                ]

    written = fetched(result, out, sem_out)
    for c, at in enumerate(chunks(own.shape[1])):
        own_copies[c].wait()
        other_copies[c].wait()

        @pl.when(left_home)
        def _():
            left_copies[c].wait()

        @pl.when(jnp.logical_not(left_home))
        def _():
            right_copies[c].wait()

        result[:, at] = product(factors[...], slab[:, at]).astype(BF16)
        written[c].start()
    for copy in written:
        copy.wait()


def gamma_block(info, early, late, own, other, following, preceding):
    rows, aux = own.shape
    return pl.pallas_call(
        gamma_kernel,
        in_specs=[SMEM] + [VMEM] * 8 + [ANY] * 4,
        out_specs=ANY,
        out_shape=jax.ShapeDtypeStruct((rows, aux), BF16),
        scratch_shapes=[
            pltpu.VMEM((3 * rows, aux), BF16),
            pltpu.VMEM((rows, aux), BF16),
            pltpu.VMEM((rows, 3 * rows), BF16),
            *[pltpu.SemaphoreType.DMA((CHUNKS,))] * 4,
        ],
        compiler_params=params(56),
        cost_estimate=pl.CostEstimate(flops=0, bytes_accessed=0, transcendentals=0),
        name="gamma_block",
    )(info, *early, *late, own, other, following, preceding)


def density_kernel(p0, p1, p2, p3, out):
    def unfolded(piece):
        wide = piece[512:544].astype(F32) + piece[544:576].astype(F32)
        turned = pltpu.roll(wide, 64, 1)
        return jnp.concatenate([wide[:, :64], turned[:, :64]], axis=0)

    out[...] = (unfolded(p0) + unfolded(p2)) + (unfolded(p1) + unfolded(p3))


def density_over_x(pieces):
    return pl.pallas_call(
        density_kernel,
        in_specs=[VMEM] * 4,
        out_specs=VMEM,
        out_shape=jax.ShapeDtypeStruct((64, 64), F32),
        compiler_params=params(8),
        cost_estimate=pl.CostEstimate(flops=0, bytes_accessed=0, transcendentals=0),
        name="density_over_x",
    )(*pieces)


def along_x(value, by):
    return lax.ppermute(
        value, "aux", [(a, a // X * X + (a + by) % X) for a in range(lax.axis_size("aux"))]
    )


def across_y(value):
    return lax.ppermute(value, "aux", [(a, a ^ X ^ 1) for a in range(lax.axis_size("aux"))])


def from_cores(core, value, occ_to, aux_to=lambda a: a):
    aux, occ = lax.axis_size("aux"), lax.axis_size("occ")
    return lax.ppermute(
        value,
        ("aux", "occ"),
        [
            (a * occ + k, aux_to(a) * occ + occ_to(k) % occ)
            for a in range(aux)
            for k in range(core, occ, 2)
        ],
    )


def swapped(value, axis, other):
    return lax.ppermute(value, axis, [(k, other(k)) for k in range(lax.axis_size(axis))])


def together(values):
    return lax.optimization_barrier(tuple(values))


def after(value, *earlier):
    return lax.optimization_barrier((value, *earlier))[0]


def body(orbital_slabs, occ_energy, virt_energy, pair_kept):
    occ_count, virt_count, aux_count = orbital_slabs.shape
    rows = occ_count * virt_count
    occ = lax.axis_size("occ")
    slabs = orbital_slabs.reshape(rows, aux_count)
    place = lax.axis_index("occ")
    core = lax.rem(place, 2)
    aux_place = lax.axis_index("aux")
    x = lax.rem(aux_place, X)
    info = jnp.stack([core, x, aux_place // X]).astype(jnp.int32)

    following = lax.ppermute(slabs, "occ", [(k, (k - 1) % occ) for k in range(0, occ, 2)])
    other = swapped(slabs, "occ", lambda k: k ^ 1)
    inner_energy = swapped(occ_energy, "occ", lambda k: k ^ 1)
    aux = lax.axis_size("aux")
    outer_energy = lax.ppermute(
        inner_energy,
        ("aux", "occ"),
        [
            (a * occ + k, (a ^ 1) * occ + (k + (2 if k % 2 == 0 else -2)) % occ)
            for a in range(aux)
            for k in range(occ)
        ],
    )
    along = jnp.tile(virt_energy.astype(F32), 2).reshape(1, Q)
    keep_in = pair_kept[place - core].astype(F32)
    keep_out = pair_kept[lax.rem(place - 1 + core + occ, occ)].astype(F32)

    pieces = early_integrals(info, after(slabs, inner_energy, along), other)
    *arrived, outer_energy = together([*(along_x(pieces[d], d) for d in (1, 2, 3)), outer_energy])
    table = jnp.concatenate(
        [occ_energy, inner_energy, outer_energy, jnp.stack([keep_in, keep_out]).astype(BF16)]
    ).astype(F32)
    sums = pieces[0].astype(F32)
    for value in arrived:
        sums = sums + value.astype(F32)
    scattered = sums.astype(BF16)
    sums = scattered.astype(F32) + across_y(scattered).astype(F32)
    inner_other = swapped(sums[Q:], "occ", lambda k: k ^ 1)
    tilde, density = early_tilde(info, table, sums, inner_other, along)
    early = [tilde, *together(along_x(tilde, d) for d in (1, 2, 3))]

    following = after(following, sums)
    preceding = lax.ppermute(
        after(slabs, following), "occ", [(k, (k + 1) % occ) for k in range(1, occ, 2)]
    )
    pieces = late_integrals(info, slabs, following)
    arrived = together(
        from_cores(1, pieces[d], lambda k: k - 1, lambda a, d=d: a // X * X + (a + d) % X)
        for d in range(X)
    )
    sums = arrived[0].astype(F32)
    for value in arrived[1:]:
        sums = sums + value.astype(F32)
    sums = sums.astype(BF16)
    shares = together(
        [
            from_cores(0, sums, lambda k: k + 2, lambda a: a ^ 2),
            from_cores(0, sums, lambda k: k + 2, lambda a: a ^ X ^ 3),
            from_cores(0, sums, lambda k: k + 1, lambda a: a ^ X ^ 1),
            from_cores(0, sums, lambda k: k + 1),
        ]
    )
    tilde = late_tilde(info, table, *shares, density, along)
    late = [tilde, *together(along_x(tilde, d) for d in (1, 2, 3))]

    density = density_over_x(late)
    for bit in (4, 8, 16, 2, 1):
        if bit == 16:
            density = after(density, preceding)
        density = density + swapped(density, "occ", lambda k, bit=bit: k ^ bit)
    virt_density = density / (4.0 * occ_count * occ_count * virt_count)

    gamma = gamma_block(info, early, late, slabs, other, following, preceding)
    return gamma.reshape(occ_count, virt_count, aux_count), virt_density


def solution(mesh):
    return jax.shard_map(
        body,
        mesh=mesh,
        in_specs=(P("occ", None, "aux"), P("occ"), P(), P()),
        out_specs=(P("occ", None, "aux"), P()),
        check_vma=False,
    )
```

```python
import functools

import jax
import jax.numpy as jnp
from jax import lax
from jax.experimental import pallas as pl
from jax.experimental.pallas import tpu as pltpu
from jax.sharding import PartitionSpec as P

F32 = jnp.float32
BF16 = jnp.bfloat16
MIB = 1 << 20
X = 4
CHUNKS = 4
SMEM = pl.BlockSpec(memory_space=pltpu.SMEM)
VMEM = pl.BlockSpec(memory_space=pltpu.VMEM)
ANY = pl.BlockSpec(memory_space=pl.ANY)
Q = 128


def params(mib):
    return pltpu.CompilerParams(vmem_limit_bytes=mib * MIB)


def rows_product(left, right):
    return lax.dot_general(left, right, (((1,), (1,)), ((), ())), preferred_element_type=F32)


def product(left, right):
    return lax.dot_general(left, right, (((1,), (0,)), ((), ())), preferred_element_type=F32)


def owned(info, x):
    return x ^ info[2]


def owned_late(info, x):
    return x ^ info[2] ^ (1 - info[0])


def chunks(aux):
    width = aux // CHUNKS
    return [slice(c * width, (c + 1) * width) for c in range(CHUNKS)]


def fetched(source, target, semaphores):
    return [
        pltpu.make_async_copy(source.at[:, at], target.at[:, at], semaphores.at[c])
        for c, at in enumerate(chunks(source.shape[1]))
    ]


def early_integrals_kernel(
    info, own, other, o0, o1, o2, o3, mine, theirs, total_own, total_inner, sem_mine, sem_theirs
):
    own_copies = fetched(own, mine, sem_mine)
    other_copies = fetched(other, theirs, sem_theirs)
    for copy in own_copies + other_copies:
        copy.start()

    def add(total, value, first):
        if first:
            total[...] = value
        else:
            total[...] += value

    for c, at in enumerate(chunks(own.shape[1])):
        own_copies[c].wait()
        add(total_own, rows_product(mine[:, at], mine[:, at]), c == 0)

    def half(block, at, parity):
        return jnp.concatenate(
            [block[(2 * q + parity) * 64 : (2 * q + parity + 1) * 64, at] for q in range(4)], axis=0
        )

    for c, at in enumerate(chunks(own.shape[1])):
        other_copies[c].wait()

        @pl.when(info[0] == 0)
        def _():
            add(total_inner, rows_product(half(mine, at, 0), theirs[:, at]), c == 0)

        @pl.when(info[0] == 1)
        def _():
            add(total_inner, rows_product(half(theirs, at, 1), mine[:, at]), c == 0)

    for d, out in enumerate((o0, o1, o2, o3)):
        q = owned(info, lax.rem(info[1] + d, X))
        out[0:128, :] = total_own[pl.ds(pl.multiple_of(q * 128, 128), 128), :].astype(BF16)
        out[128:192, :] = total_inner[pl.ds(pl.multiple_of(q * 64, 64), 64), :].astype(BF16)


def early_integrals(info, own, other):
    rows, aux = own.shape
    return pl.pallas_call(
        early_integrals_kernel,
        in_specs=[SMEM, ANY, ANY],
        out_specs=[VMEM] * 4,
        out_shape=[jax.ShapeDtypeStruct((192, rows), BF16)] * 4,
        scratch_shapes=[
            pltpu.VMEM((rows, aux), BF16),
            pltpu.VMEM((rows, aux), BF16),
            pltpu.VMEM((rows, rows), F32),
            pltpu.VMEM((rows // 2, rows), F32),
            pltpu.SemaphoreType.DMA((CHUNKS,)),
            pltpu.SemaphoreType.DMA((CHUNKS,)),
        ],
        compiler_params=params(60),
        cost_estimate=pl.CostEstimate(flops=0, bytes_accessed=0, transcendentals=0),
        name="early_integrals",
    )(info, own, other)


def late_integrals_kernel(
    info, own, following, o0, o1, o2, o3, mine, theirs, total, sem_mine, sem_theirs
):
    @pl.when(info[0] == 1)
    def _():
        own_copies = fetched(own, mine, sem_mine)
        other_copies = fetched(following, theirs, sem_theirs)
        for pair in zip(own_copies, other_copies):
            for copy in pair:
                copy.start()
        for c, at in enumerate(chunks(own.shape[1])):
            own_copies[c].wait()
            other_copies[c].wait()
            value = rows_product(mine[:, at], theirs[:, at])
            if c == 0:
                total[...] = value
            else:
                total[...] += value
        for d, out in enumerate((o0, o1, o2, o3)):
            q = owned(info, lax.rem(info[1] + d, X))
            out[...] = total[pl.ds(pl.multiple_of(q * 128, 128), 128), :].astype(BF16)

    @pl.when(info[0] == 0)
    def _():
        for out in (o0, o1, o2, o3):
            out[...] = jnp.zeros_like(out)


def late_integrals(info, own, following):
    rows, aux = own.shape
    return pl.pallas_call(
        late_integrals_kernel,
        in_specs=[SMEM, ANY, ANY],
        out_specs=[VMEM] * 4,
        out_shape=[jax.ShapeDtypeStruct((Q, rows), BF16)] * 4,
        scratch_shapes=[
            pltpu.VMEM((rows, aux), BF16),
            pltpu.VMEM((rows, aux), BF16),
            pltpu.VMEM((rows, rows), F32),
            pltpu.SemaphoreType.DMA((CHUNKS,)),
            pltpu.SemaphoreType.DMA((CHUNKS,)),
        ],
        compiler_params=params(56),
        cost_estimate=pl.CostEstimate(flops=0, bytes_accessed=0, transcendentals=0),
        name="late_integrals",
    )(info, own, following)


def block_transposed(wide):
    turned = wide.T
    top, bottom = turned[:64], turned[64:]
    low = lax.broadcasted_iota(jnp.int32, (64, 128), 1) < 64
    first = jnp.where(low, top, pltpu.roll(bottom, 64, 1))
    second = jnp.where(low, pltpu.roll(top, 64, 1), bottom)
    return jnp.concatenate([first, second], axis=0), turned


def diagonal_blocks(square):
    return square[:64, :64] + pltpu.roll(square[64:, :], 64, 1)[:, :64]


def tilde_rows(integrals, q, left, right, virt, keep, store):
    first = jnp.zeros((128, 128), F32)
    second = jnp.zeros((128, 128), F32)
    upper = lax.broadcasted_iota(jnp.int32, (128, 1), 0) < 64
    lower = lax.broadcasted_iota(jnp.int32, (1, 128), 1) < 64
    along = jnp.concatenate([virt, virt], axis=1).astype(F32)
    down = jnp.broadcast_to(along, (128, 128)).T
    gap_left = jnp.where(upper, left(2 * q), left(2 * q + 1)) - down
    for J in range(4):
        at = slice(J * 128, (J + 1) * 128)
        gap_right = jnp.where(lower, right(2 * J), right(2 * J + 1)) - along
        amp = (keep * integrals(at) / (gap_left + gap_right)).astype(BF16)
        wide = amp.astype(F32)
        swapped, turned = block_transposed(wide)
        tilde_wide = (2.0 * wide - swapped).astype(BF16).astype(F32)
        tilde = tilde_wide.astype(BF16)
        tilde_turned = tilde_wide.T.astype(BF16)
        first += rows_product(tilde, amp)
        second += rows_product(tilde_turned, turned.astype(BF16))
        store(J, tilde, tilde_turned)
    return diagonal_blocks(first), diagonal_blocks(second)


def early_tilde_kernel(
    info, kept, own_energy, inner_energy, here, there, inner_mine, inner_other, virt, out, density
):
    q = owned(info, info[1])
    left_home = info[0] == 0

    def own(i):
        return own_energy[i]

    def left(i):
        return jnp.where(left_home, own_energy[i], inner_energy[i])

    def right(j):
        return jnp.where(left_home, inner_energy[j], own_energy[j])

    def store_own(J, tilde, turned):
        out[J] = tilde

    own_first, _ = tilde_rows(
        lambda at: here[0:128, at].astype(F32) + there[0:128, at].astype(F32), q, own, own, virt[...], 1.0, store_own
    )

    def inner(at):
        mine, theirs = inner_mine[:, at], inner_other[:, at]
        return jnp.concatenate(
            [jnp.where(left_home, mine, theirs), jnp.where(left_home, theirs, mine)], axis=0
        )

    def store_inner(J, tilde, turned):
        out[4 + J] = jnp.where(left_home, tilde, turned)

    first, second = tilde_rows(
        inner, q, left, right, virt[...], kept[info[3] - info[0]].astype(F32), store_inner
    )
    density[...] = own_first + jnp.where(left_home, first + second, 0.0)


def early_tilde(*operands):
    return pl.pallas_call(
        early_tilde_kernel,
        in_specs=[SMEM] * 4 + [VMEM] * 5,
        out_specs=[VMEM, VMEM],
        out_shape=[jax.ShapeDtypeStruct((8, 128, 128), BF16), jax.ShapeDtypeStruct((64, 64), F32)],
        compiler_params=pltpu.CompilerParams(vmem_limit_bytes=32 * MIB),
        cost_estimate=pl.CostEstimate(flops=0, bytes_accessed=0, transcendentals=0),
        name="early_tilde",
    )(*operands)


def late_tilde_kernel(
    info, kept, left_energy, right_energy, mine, partner, early, virt, straight, turned, density
):
    def outer(at):
        return mine[:, at].astype(F32) + partner[:, at].astype(F32)

    def left(i):
        return left_energy[i]

    def right(j):
        return right_energy[j]

    def store(J, tilde, tilde_turned):
        straight[J * 128 : (J + 1) * 128, :] = tilde
        turned[J * 128 : (J + 1) * 128, :] = tilde_turned

    first, second = tilde_rows(
        outer, owned(info, info[1]), left, right, virt[...], kept[info[3] - info[0] + 1].astype(F32), store
    )
    density[...] = early[...] + jnp.where(info[0] == 0, first + second, 0.0)


def late_tilde(*operands):
    return pl.pallas_call(
        late_tilde_kernel,
        in_specs=[SMEM] * 4 + [VMEM] * 4,
        out_specs=[VMEM] * 3,
        out_shape=[
            jax.ShapeDtypeStruct((512, 128), BF16),
            jax.ShapeDtypeStruct((512, 128), BF16),
            jax.ShapeDtypeStruct((64, 64), F32),
        ],
        compiler_params=params(32),
        cost_estimate=pl.CostEstimate(flops=0, bytes_accessed=0, transcendentals=0),
        name="late_tilde",
    )(*operands)


def gamma_kernel(
    info, e0, e1, e2, e3, p0, p1, p2, p3, own, other, following, preceding, out,
    slab, result, factors, sem_own, sem_other, sem_outer, sem_out,
):
    rows = own.shape[0]
    left_home = info[0] == 1
    own_copies = fetched(own, slab.at[:rows], sem_own)
    other_copies = fetched(other, slab.at[rows : 2 * rows], sem_other)
    left_copies = fetched(following, slab.at[2 * rows :], sem_outer)
    right_copies = fetched(preceding, slab.at[2 * rows :], sem_outer)
    for c in range(CHUNKS):
        own_copies[c].start()
        other_copies[c].start()

        @pl.when(left_home)
        def _():
            left_copies[c].start()

        @pl.when(jnp.logical_not(left_home))
        def _():
            right_copies[c].start()

    for d, (early, late) in enumerate(((e0, p0), (e1, p1), (e2, p2), (e3, p3))):
        q = owned(info, lax.rem(info[1] + X - d, X))
        here = pl.ds(pl.multiple_of(q * 128, 128), 128)
        for J in range(4):
            factors[here, J * 128 : (J + 1) * 128] = early[J]

        q_late = owned_late(info, lax.rem(info[1] + X - d, X))
        here_late = pl.ds(pl.multiple_of(q_late * 128, 128), 128)

        @pl.when(jnp.logical_not(left_home))
        def _():
            column = pl.ds(pl.multiple_of(2 * rows + q_late * 128, 128), 128)
            for J in range(4):
                factors[here, rows + J * 128 : rows + (J + 1) * 128] = early[4 + J]
                factors[J * 128 : (J + 1) * 128, column] = late[J * 128 : (J + 1) * 128]

        @pl.when(left_home)
        def _():
            column = pl.ds(pl.multiple_of(rows + q * 128, 128), 128)
            for J in range(4):
                factors[J * 128 : (J + 1) * 128, column] = early[4 + J]
                factors[here_late, 2 * rows + J * 128 : 2 * rows + (J + 1) * 128] = late[
                    J * 128 : (J + 1) * 128
                ]

    written = fetched(result, out, sem_out)
    for c, at in enumerate(chunks(own.shape[1])):
        own_copies[c].wait()
        other_copies[c].wait()

        @pl.when(left_home)
        def _():
            left_copies[c].wait()

        @pl.when(jnp.logical_not(left_home))
        def _():
            right_copies[c].wait()

        result[:, at] = product(factors[...], slab[:, at]).astype(BF16)
        written[c].start()
    for copy in written:
        copy.wait()


def gamma_block(info, early, late, own, other, following, preceding):
    rows, aux = own.shape
    return pl.pallas_call(
        gamma_kernel,
        in_specs=[SMEM] + [VMEM] * 8 + [ANY] * 4,
        out_specs=ANY,
        out_shape=jax.ShapeDtypeStruct((rows, aux), BF16),
        scratch_shapes=[
            pltpu.VMEM((3 * rows, aux), BF16),
            pltpu.VMEM((rows, aux), BF16),
            pltpu.VMEM((rows, 3 * rows), BF16),
            *[pltpu.SemaphoreType.DMA((CHUNKS,))] * 4,
        ],
        compiler_params=params(56),
        cost_estimate=pl.CostEstimate(flops=0, bytes_accessed=0, transcendentals=0),
        name="gamma_block",
    )(info, *early, *late, own, other, following, preceding)


def along_x(value, by):
    return lax.ppermute(
        value, "aux", [(a, a // X * X + (a + by) % X) for a in range(lax.axis_size("aux"))]
    )


def across_y(value):
    return lax.ppermute(value, "aux", [(a, a ^ X ^ 1) for a in range(lax.axis_size("aux"))])


def from_cores(core, value, occ_to, aux_to=lambda a: a):
    aux, occ = lax.axis_size("aux"), lax.axis_size("occ")
    return lax.ppermute(
        value,
        ("aux", "occ"),
        [
            (a * occ + k, aux_to(a) * occ + occ_to(k) % occ)
            for a in range(aux)
            for k in range(core, occ, 2)
        ],
    )


def swapped(value, axis, other):
    return lax.ppermute(value, axis, [(k, other(k)) for k in range(lax.axis_size(axis))])


def together(values):
    return lax.optimization_barrier(tuple(values))


def after(value, *earlier):
    return lax.optimization_barrier((value, *earlier))[0]


def body(orbital_slabs, occ_energy, virt_energy, pair_kept):
    occ_count, virt_count, aux_count = orbital_slabs.shape
    rows = occ_count * virt_count
    occ = lax.axis_size("occ")
    slabs = orbital_slabs.reshape(rows, aux_count)
    place = lax.axis_index("occ")
    core = lax.rem(place, 2)
    aux_place = lax.axis_index("aux")
    x = lax.rem(aux_place, X)
    info = jnp.stack([core, x, aux_place // X, place]).astype(jnp.int32)
    energy = occ_energy.astype(F32)

    following = lax.ppermute(slabs, "occ", [(k, (k - 1) % occ) for k in range(0, occ, 2)])
    other = swapped(slabs, "occ", lambda k: k ^ 1)
    inner_energy = swapped(energy, "occ", lambda k: k ^ 1)
    outer_energy = from_cores(1, inner_energy, lambda k: k - 3, lambda a: a ^ 1)
    virt = virt_energy.reshape(1, virt_count)

    pieces = early_integrals(info, slabs, other)
    arrived = together(along_x(pieces[d], d) for d in (1, 2, 3))
    sums = pieces[0].astype(F32)
    for value in arrived:
        sums = sums + value.astype(F32)
    scattered = sums.astype(BF16)
    there, outer_energy = together([across_y(scattered), outer_energy])
    inner = scattered[Q:].astype(F32) + there[Q:].astype(F32)
    inner_other = swapped(inner, "occ", lambda k: k ^ 1)
    tilde, density = early_tilde(
        info, pair_kept, energy, inner_energy, scattered, there, inner, inner_other, virt
    )
    own_tilde = tilde

    following = after(following, tilde)
    pieces = late_integrals(info, slabs, following)
    preceding = lax.ppermute(
        after(slabs, pieces[0]), "occ", [(k, (k + 1) % occ) for k in range(1, occ, 2)]
    )
    arrived = together(
        from_cores(1, pieces[d], lambda k: k - 1, lambda a, d=d: a // X * X + (a + d) % X)
        for d in range(X)
    )
    sums = arrived[0].astype(F32)
    for value in arrived[1:]:
        sums = sums + value.astype(F32)
    sums = sums.astype(BF16)
    partner = from_cores(0, sums, lambda k: k, lambda a: a ^ X ^ 1)
    straight, turned, density = late_tilde(
        info, pair_kept, inner_energy, outer_energy, sums, partner, density, virt
    )
    left = from_cores(0, straight, lambda k: k + 1)
    right = from_cores(0, turned, lambda k: k + 2, lambda a: a ^ 1)

    tilde = jnp.where(core == 1, left, right)
    own_tilde = after(own_tilde, left)
    early = [own_tilde, *together(along_x(own_tilde, d) for d in (1, 2, 3))]
    late = [tilde, *together(along_x(tilde, d) for d in (1, 2, 3))]
    gamma = gamma_block(info, early, late, slabs, other, following, preceding)

    for flip, earlier in ((4, ()), (8, (left,)), (16, (early[1],)), (2, (preceding, tilde))):
        density = after(density, *earlier)
        density = density + swapped(density, "occ", lambda k, flip=flip: k ^ flip)
    parts = [along_x(density, d) for d in range(1, X)]
    gamma, density, *parts = together([gamma, density, *parts])
    density = (density + parts[1]) + (parts[0] + parts[2])
    density = density + swapped(density, "occ", lambda k: k ^ 1)
    virt_density = density / (4.0 * occ_count * occ_count * virt_count)
    return gamma.reshape(occ_count, virt_count, aux_count), virt_density


def solution(mesh):
    return jax.shard_map(
        body,
        mesh=mesh,
        in_specs=(P("occ", None, "aux"), P("occ"), P(), P()),
        out_specs=(P("occ", None, "aux"), P()),
        check_vma=False,
    )
```

```python
import functools

import jax
import jax.numpy as jnp
from jax import lax
from jax.experimental import pallas as pl
from jax.experimental.pallas import tpu as pltpu
from jax.sharding import PartitionSpec as P

F32 = jnp.float32
BF16 = jnp.bfloat16
MIB = 1 << 20
X = 4
CHUNKS = 3
SMEM = pl.BlockSpec(memory_space=pltpu.SMEM)
VMEM = pl.BlockSpec(memory_space=pltpu.VMEM)
ANY = pl.BlockSpec(memory_space=pl.ANY)
Q = 128


def params(mib):
    return pltpu.CompilerParams(vmem_limit_bytes=mib * MIB)


def rows_product(left, right):
    return lax.dot_general(left, right, (((1,), (1,)), ((), ())), preferred_element_type=F32)


def product(left, right):
    return lax.dot_general(left, right, (((1,), (0,)), ((), ())), preferred_element_type=F32)


def owned(info, x):
    return x ^ info[2]


def owned_late(info, x):
    return x ^ info[2] ^ (1 - info[0])


def chunks(aux):
    width = aux // CHUNKS
    return [slice(c * width, (c + 1) * width) for c in range(CHUNKS)]


def fetched(source, target, semaphores):
    return [
        pltpu.make_async_copy(source.at[:, at], target.at[:, at], semaphores.at[c])
        for c, at in enumerate(chunks(source.shape[1]))
    ]


def early_integrals_kernel(
    info, own, other, o0, o1, o2, o3, mine, theirs, total_own, total_inner, sem_mine, sem_theirs
):
    own_copies = fetched(own, mine, sem_mine)
    other_copies = fetched(other, theirs, sem_theirs)
    for copy in own_copies + other_copies:
        copy.start()

    def add(total, value, first):
        if first:
            total[...] = value
        else:
            total[...] += value

    for c, at in enumerate(chunks(own.shape[1])):
        own_copies[c].wait()
        add(total_own, rows_product(mine[:, at], mine[:, at]), c == 0)

    def half(block, at, parity):
        return jnp.concatenate(
            [block[(2 * q + parity) * 64 : (2 * q + parity + 1) * 64, at] for q in range(4)], axis=0
        )

    for c, at in enumerate(chunks(own.shape[1])):
        other_copies[c].wait()

        @pl.when(info[0] == 0)
        def _():
            add(total_inner, rows_product(half(mine, at, 0), theirs[:, at]), c == 0)

        @pl.when(info[0] == 1)
        def _():
            add(total_inner, rows_product(half(theirs, at, 1), mine[:, at]), c == 0)

    for d, out in enumerate((o0, o1, o2, o3)):
        q = owned(info, lax.rem(info[1] + d, X))
        out[0:128, :] = total_own[pl.ds(pl.multiple_of(q * 128, 128), 128), :].astype(BF16)
        out[128:192, :] = total_inner[pl.ds(pl.multiple_of(q * 64, 64), 64), :].astype(BF16)


def early_integrals(info, own, other):
    rows, aux = own.shape
    return pl.pallas_call(
        early_integrals_kernel,
        in_specs=[SMEM, ANY, ANY],
        out_specs=[VMEM] * 4,
        out_shape=[jax.ShapeDtypeStruct((192, rows), BF16)] * 4,
        scratch_shapes=[
            pltpu.VMEM((rows, aux), BF16),
            pltpu.VMEM((rows, aux), BF16),
            pltpu.VMEM((rows, rows), F32),
            pltpu.VMEM((rows // 2, rows), F32),
            pltpu.SemaphoreType.DMA((CHUNKS,)),
            pltpu.SemaphoreType.DMA((CHUNKS,)),
        ],
        compiler_params=params(60),
        cost_estimate=pl.CostEstimate(flops=0, bytes_accessed=0, transcendentals=0),
        name="early_integrals",
    )(info, own, other)


def late_integrals_kernel(
    info, own, following, o0, o1, o2, o3, mine, theirs, total, sem_mine, sem_theirs
):
    @pl.when(info[0] == 1)
    def _():
        own_copies = fetched(own, mine, sem_mine)
        other_copies = fetched(following, theirs, sem_theirs)
        for pair in zip(own_copies, other_copies):
            for copy in pair:
                copy.start()
        for c, at in enumerate(chunks(own.shape[1])):
            own_copies[c].wait()
            other_copies[c].wait()
            value = rows_product(mine[:, at], theirs[:, at])
            if c == 0:
                total[...] = value
            else:
                total[...] += value
        for d, out in enumerate((o0, o1, o2, o3)):
            q = owned(info, lax.rem(info[1] + d, X))
            out[...] = total[pl.ds(pl.multiple_of(q * 128, 128), 128), :].astype(BF16)

    @pl.when(info[0] == 0)
    def _():
        for out in (o0, o1, o2, o3):
            out[...] = jnp.zeros_like(out)


def late_integrals(info, own, following):
    rows, aux = own.shape
    return pl.pallas_call(
        late_integrals_kernel,
        in_specs=[SMEM, ANY, ANY],
        out_specs=[VMEM] * 4,
        out_shape=[jax.ShapeDtypeStruct((Q, rows), BF16)] * 4,
        scratch_shapes=[
            pltpu.VMEM((rows, aux), BF16),
            pltpu.VMEM((rows, aux), BF16),
            pltpu.VMEM((rows, rows), F32),
            pltpu.SemaphoreType.DMA((CHUNKS,)),
            pltpu.SemaphoreType.DMA((CHUNKS,)),
        ],
        compiler_params=params(56),
        cost_estimate=pl.CostEstimate(flops=0, bytes_accessed=0, transcendentals=0),
        name="late_integrals",
    )(info, own, following)


def block_transposed(wide):
    turned = wide.T
    top, bottom = turned[:64], turned[64:]
    low = lax.broadcasted_iota(jnp.int32, (64, 128), 1) < 64
    first = jnp.where(low, top, pltpu.roll(bottom, 64, 1))
    second = jnp.where(low, pltpu.roll(top, 64, 1), bottom)
    return jnp.concatenate([first, second], axis=0), turned


def diagonal_blocks(square):
    return square[:64, :64] + pltpu.roll(square[64:, :], 64, 1)[:, :64]


def tilde_rows(integrals, q, left, right, virt, keep, store):
    first = jnp.zeros((128, 128), F32)
    second = jnp.zeros((128, 128), F32)
    upper = lax.broadcasted_iota(jnp.int32, (128, 1), 0) < 64
    lower = lax.broadcasted_iota(jnp.int32, (1, 128), 1) < 64
    along = jnp.concatenate([virt, virt], axis=1).astype(F32)
    down = jnp.broadcast_to(along, (128, 128)).T
    gap_left = jnp.where(upper, left(2 * q), left(2 * q + 1)) - down
    for J in range(4):
        at = slice(J * 128, (J + 1) * 128)
        gap_right = jnp.where(lower, right(2 * J), right(2 * J + 1)) - along
        amp = (keep * integrals(at) / (gap_left + gap_right)).astype(BF16)
        wide = amp.astype(F32)
        swapped, turned = block_transposed(wide)
        tilde_wide = (2.0 * wide - swapped).astype(BF16).astype(F32)
        tilde = tilde_wide.astype(BF16)
        tilde_turned = tilde_wide.T.astype(BF16)
        first += rows_product(tilde, amp)
        second += rows_product(tilde_turned, turned.astype(BF16))
        store(J, tilde, tilde_turned)
    return diagonal_blocks(first), diagonal_blocks(second)


def early_tilde_kernel(
    info, kept, own_energy, inner_energy, here, there, inner_mine, inner_other, virt, out, density
):
    q = owned(info, info[1])
    left_home = info[0] == 0

    def own(i):
        return own_energy[i]

    def left(i):
        return jnp.where(left_home, own_energy[i], inner_energy[i])

    def right(j):
        return jnp.where(left_home, inner_energy[j], own_energy[j])

    def store_own(J, tilde, turned):
        out[J] = tilde

    own_first, _ = tilde_rows(
        lambda at: here[0:128, at].astype(F32) + there[0:128, at].astype(F32), q, own, own, virt[...], 1.0, store_own
    )

    def inner(at):
        mine, theirs = inner_mine[:, at], inner_other[:, at]
        return jnp.concatenate(
            [jnp.where(left_home, mine, theirs), jnp.where(left_home, theirs, mine)], axis=0
        )

    def store_inner(J, tilde, turned):
        out[4 + J] = jnp.where(left_home, tilde, turned)

    first, second = tilde_rows(
        inner, q, left, right, virt[...], kept[info[3] - info[0]].astype(F32), store_inner
    )
    density[...] = own_first + jnp.where(left_home, first + second, 0.0)


def early_tilde(*operands):
    return pl.pallas_call(
        early_tilde_kernel,
        in_specs=[SMEM] * 4 + [VMEM] * 5,
        out_specs=[VMEM, VMEM],
        out_shape=[jax.ShapeDtypeStruct((8, 128, 128), BF16), jax.ShapeDtypeStruct((64, 64), F32)],
        compiler_params=pltpu.CompilerParams(vmem_limit_bytes=32 * MIB),
        cost_estimate=pl.CostEstimate(flops=0, bytes_accessed=0, transcendentals=0),
        name="early_tilde",
    )(*operands)


def late_tilde_kernel(
    info, kept, left_energy, right_energy, mine, partner, early, virt, straight, turned, density
):
    def outer(at):
        return mine[:, at].astype(F32) + partner[:, at].astype(F32)

    def left(i):
        return left_energy[i]

    def right(j):
        return right_energy[j]

    def store(J, tilde, tilde_turned):
        straight[J * 128 : (J + 1) * 128, :] = tilde
        turned[J * 128 : (J + 1) * 128, :] = tilde_turned

    first, second = tilde_rows(
        outer, owned(info, info[1]), left, right, virt[...], kept[info[3] - info[0] + 1].astype(F32), store
    )
    density[...] = early[...] + jnp.where(info[0] == 0, first + second, 0.0)


def late_tilde(*operands):
    return pl.pallas_call(
        late_tilde_kernel,
        in_specs=[SMEM] * 4 + [VMEM] * 4,
        out_specs=[VMEM] * 3,
        out_shape=[
            jax.ShapeDtypeStruct((512, 128), BF16),
            jax.ShapeDtypeStruct((512, 128), BF16),
            jax.ShapeDtypeStruct((64, 64), F32),
        ],
        compiler_params=params(32),
        cost_estimate=pl.CostEstimate(flops=0, bytes_accessed=0, transcendentals=0),
        name="late_tilde",
    )(*operands)


def gamma_kernel(
    info, e0, e1, e2, e3, p0, p1, p2, p3, own, other, following, preceding, out,
    slab, result, factors, sem_own, sem_other, sem_outer, sem_out,
):
    rows = own.shape[0]
    left_home = info[0] == 1
    own_copies = fetched(own, slab.at[:rows], sem_own)
    other_copies = fetched(other, slab.at[rows : 2 * rows], sem_other)
    left_copies = fetched(following, slab.at[2 * rows :], sem_outer)
    right_copies = fetched(preceding, slab.at[2 * rows :], sem_outer)
    for c in range(CHUNKS):
        own_copies[c].start()
        other_copies[c].start()

        @pl.when(left_home)
        def _():
            left_copies[c].start()

        @pl.when(jnp.logical_not(left_home))
        def _():
            right_copies[c].start()

    for d, (early, late) in enumerate(((e0, p0), (e1, p1), (e2, p2), (e3, p3))):
        q = owned(info, lax.rem(info[1] + X - d, X))
        here = pl.ds(pl.multiple_of(q * 128, 128), 128)
        for J in range(4):
            factors[here, J * 128 : (J + 1) * 128] = early[J]

        q_late = owned_late(info, lax.rem(info[1] + X - d, X))
        here_late = pl.ds(pl.multiple_of(q_late * 128, 128), 128)

        @pl.when(jnp.logical_not(left_home))
        def _():
            column = pl.ds(pl.multiple_of(2 * rows + q_late * 128, 128), 128)
            for J in range(4):
                factors[here, rows + J * 128 : rows + (J + 1) * 128] = early[4 + J]
                factors[J * 128 : (J + 1) * 128, column] = late[J * 128 : (J + 1) * 128]

        @pl.when(left_home)
        def _():
            column = pl.ds(pl.multiple_of(rows + q * 128, 128), 128)
            for J in range(4):
                factors[J * 128 : (J + 1) * 128, column] = early[4 + J]
                factors[here_late, 2 * rows + J * 128 : 2 * rows + (J + 1) * 128] = late[
                    J * 128 : (J + 1) * 128
                ]

    written = fetched(result, out, sem_out)
    for c, at in enumerate(chunks(own.shape[1])):
        own_copies[c].wait()
        other_copies[c].wait()

        @pl.when(left_home)
        def _():
            left_copies[c].wait()

        @pl.when(jnp.logical_not(left_home))
        def _():
            right_copies[c].wait()

        result[:, at] = product(factors[...], slab[:, at]).astype(BF16)
        written[c].start()
    for copy in written:
        copy.wait()


def gamma_block(info, early, late, own, other, following, preceding):
    rows, aux = own.shape
    return pl.pallas_call(
        gamma_kernel,
        in_specs=[SMEM] + [VMEM] * 8 + [ANY] * 4,
        out_specs=ANY,
        out_shape=jax.ShapeDtypeStruct((rows, aux), BF16),
        scratch_shapes=[
            pltpu.VMEM((3 * rows, aux), BF16),
            pltpu.VMEM((rows, aux), BF16),
            pltpu.VMEM((rows, 3 * rows), BF16),
            *[pltpu.SemaphoreType.DMA((CHUNKS,))] * 4,
        ],
        compiler_params=params(56),
        cost_estimate=pl.CostEstimate(flops=0, bytes_accessed=0, transcendentals=0),
        name="gamma_block",
    )(info, *early, *late, own, other, following, preceding)


def along_x(value, by):
    return lax.ppermute(
        value, "aux", [(a, a // X * X + (a + by) % X) for a in range(lax.axis_size("aux"))]
    )


def across_y(value):
    return lax.ppermute(value, "aux", [(a, a ^ X ^ 1) for a in range(lax.axis_size("aux"))])


def from_cores(core, value, occ_to, aux_to=lambda a: a):
    aux, occ = lax.axis_size("aux"), lax.axis_size("occ")
    return lax.ppermute(
        value,
        ("aux", "occ"),
        [
            (a * occ + k, aux_to(a) * occ + occ_to(k) % occ)
            for a in range(aux)
            for k in range(core, occ, 2)
        ],
    )


def swapped(value, axis, other):
    return lax.ppermute(value, axis, [(k, other(k)) for k in range(lax.axis_size(axis))])


def together(values):
    return lax.optimization_barrier(tuple(values))


def after(value, *earlier):
    return lax.optimization_barrier((value, *earlier))[0]


def body(orbital_slabs, occ_energy, virt_energy, pair_kept):
    occ_count, virt_count, aux_count = orbital_slabs.shape
    rows = occ_count * virt_count
    occ = lax.axis_size("occ")
    slabs = orbital_slabs.reshape(rows, aux_count)
    place = lax.axis_index("occ")
    core = lax.rem(place, 2)
    aux_place = lax.axis_index("aux")
    x = lax.rem(aux_place, X)
    info = jnp.stack([core, x, aux_place // X, place]).astype(jnp.int32)
    energy = occ_energy.astype(F32)

    following = lax.ppermute(slabs, "occ", [(k, (k - 1) % occ) for k in range(0, occ, 2)])
    other = swapped(slabs, "occ", lambda k: k ^ 1)
    inner_energy = swapped(energy, "occ", lambda k: k ^ 1)
    outer_energy = from_cores(1, inner_energy, lambda k: k - 3, lambda a: a ^ 1)
    virt = virt_energy.reshape(1, virt_count)

    pieces = early_integrals(info, slabs, other)
    arrived = together(along_x(pieces[d], d) for d in (1, 2, 3))
    sums = pieces[0].astype(F32)
    for value in arrived:
        sums = sums + value.astype(F32)
    scattered = sums.astype(BF16)
    there, outer_energy = together([across_y(scattered), outer_energy])
    inner = scattered[Q:].astype(F32) + there[Q:].astype(F32)
    inner_other = swapped(inner, "occ", lambda k: k ^ 1)
    tilde, density = early_tilde(
        info, pair_kept, energy, inner_energy, scattered, there, inner, inner_other, virt
    )
    own_tilde = tilde

    following = after(following, tilde)
    pieces = late_integrals(info, slabs, following)
    preceding = lax.ppermute(
        after(slabs, pieces[0]), "occ", [(k, (k + 1) % occ) for k in range(1, occ, 2)]
    )
    arrived = together(
        from_cores(1, pieces[d], lambda k: k - 1, lambda a, d=d: a // X * X + (a + d) % X)
        for d in range(X)
    )
    sums = arrived[0].astype(F32)
    for value in arrived[1:]:
        sums = sums + value.astype(F32)
    sums = sums.astype(BF16)
    partner = from_cores(0, sums, lambda k: k, lambda a: a ^ X ^ 1)
    straight, turned, density = late_tilde(
        info, pair_kept, inner_energy, outer_energy, sums, partner, density, virt
    )
    left = from_cores(0, straight, lambda k: k + 1)
    right = from_cores(0, turned, lambda k: k + 2, lambda a: a ^ 1)

    tilde = jnp.where(core == 1, left, right)
    own_tilde = after(own_tilde, left)
    early = [own_tilde, *together(along_x(own_tilde, d) for d in (1, 2, 3))]
    late = [tilde, *together(along_x(tilde, d) for d in (1, 2, 3))]
    gamma = gamma_block(info, early, late, slabs, other, following, preceding)

    for flip, earlier in ((4, ()), (8, (left,)), (16, (early[1],)), (2, (preceding, tilde))):
        density = after(density, *earlier)
        density = density + swapped(density, "occ", lambda k, flip=flip: k ^ flip)
    parts = [along_x(density, d) for d in range(1, X)]
    gamma, density, *parts = together([gamma, density, *parts])
    density = (density + parts[1]) + (parts[0] + parts[2])
    density = density + swapped(density, "occ", lambda k: k ^ 1)
    virt_density = density / (4.0 * occ_count * occ_count * virt_count)
    return gamma.reshape(occ_count, virt_count, aux_count), virt_density


def solution(mesh):
    return jax.shard_map(
        body,
        mesh=mesh,
        in_specs=(P("occ", None, "aux"), P("occ"), P(), P()),
        out_specs=(P("occ", None, "aux"), P()),
        check_vma=False,
    )
```

```python
import functools

import jax
import jax.numpy as jnp
from jax import lax
from jax.experimental import pallas as pl
from jax.experimental.pallas import tpu as pltpu
from jax.sharding import PartitionSpec as P

F32 = jnp.float32
BF16 = jnp.bfloat16
MIB = 1 << 20
X = 4
CHUNKS = 3
SMEM = pl.BlockSpec(memory_space=pltpu.SMEM)
VMEM = pl.BlockSpec(memory_space=pltpu.VMEM)
ANY = pl.BlockSpec(memory_space=pl.ANY)
Q = 128


def params(mib):
    return pltpu.CompilerParams(vmem_limit_bytes=mib * MIB)


def rows_product(left, right):
    return lax.dot_general(left, right, (((1,), (1,)), ((), ())), preferred_element_type=F32)


def product(left, right):
    return lax.dot_general(left, right, (((1,), (0,)), ((), ())), preferred_element_type=F32)


def owned(info, x):
    return x ^ info[2]


def owned_late(info, x):
    return x ^ info[2] ^ (1 - info[0])


def chunks(aux):
    width = aux // CHUNKS
    return [slice(c * width, (c + 1) * width) for c in range(CHUNKS)]


def fetched(source, target, semaphores):
    return [
        pltpu.make_async_copy(source.at[:, at], target.at[:, at], semaphores.at[c])
        for c, at in enumerate(chunks(source.shape[1]))
    ]


def early_integrals_kernel(
    info, own, other, o0, o1, o2, o3, mine, theirs, total_own, total_inner, sem_mine, sem_theirs
):
    own_copies = fetched(own, mine, sem_mine)
    other_copies = fetched(other, theirs, sem_theirs)
    for copy in own_copies + other_copies:
        copy.start()

    def add(total, value, first):
        if first:
            total[...] = value
        else:
            total[...] += value

    for c, at in enumerate(chunks(own.shape[1])):
        own_copies[c].wait()
        add(total_own, rows_product(mine[:, at], mine[:, at]), c == 0)

    def half(block, at, parity):
        return jnp.concatenate(
            [block[(2 * q + parity) * 64 : (2 * q + parity + 1) * 64, at] for q in range(4)], axis=0
        )

    for c, at in enumerate(chunks(own.shape[1])):
        other_copies[c].wait()

        @pl.when(info[0] == 0)
        def _():
            add(total_inner, rows_product(half(mine, at, 0), theirs[:, at]), c == 0)

        @pl.when(info[0] == 1)
        def _():
            add(total_inner, rows_product(half(theirs, at, 1), mine[:, at]), c == 0)

    for d, out in enumerate((o0, o1, o2, o3)):
        q = owned(info, lax.rem(info[1] + d, X))
        out[0:128, :] = total_own[pl.ds(pl.multiple_of(q * 128, 128), 128), :].astype(BF16)
        out[128:192, :] = total_inner[pl.ds(pl.multiple_of(q * 64, 64), 64), :].astype(BF16)


def early_integrals(info, own, other):
    rows, aux = own.shape
    return pl.pallas_call(
        early_integrals_kernel,
        in_specs=[SMEM, ANY, ANY],
        out_specs=[VMEM] * 4,
        out_shape=[jax.ShapeDtypeStruct((192, rows), BF16)] * 4,
        scratch_shapes=[
            pltpu.VMEM((rows, aux), BF16),
            pltpu.VMEM((rows, aux), BF16),
            pltpu.VMEM((rows, rows), F32),
            pltpu.VMEM((rows // 2, rows), F32),
            pltpu.SemaphoreType.DMA((CHUNKS,)),
            pltpu.SemaphoreType.DMA((CHUNKS,)),
        ],
        compiler_params=params(60),
        cost_estimate=pl.CostEstimate(flops=0, bytes_accessed=0, transcendentals=0),
        name="early_integrals",
    )(info, own, other)


def late_integrals_kernel(
    info, own, following, o0, o1, o2, o3, mine, theirs, total, sem_mine, sem_theirs
):
    @pl.when(info[0] == 1)
    def _():
        own_copies = fetched(own, mine, sem_mine)
        other_copies = fetched(following, theirs, sem_theirs)
        for pair in zip(own_copies, other_copies):
            for copy in pair:
                copy.start()
        for c, at in enumerate(chunks(own.shape[1])):
            own_copies[c].wait()
            other_copies[c].wait()
            value = rows_product(mine[:, at], theirs[:, at])
            if c == 0:
                total[...] = value
            else:
                total[...] += value
        for d, out in enumerate((o0, o1, o2, o3)):
            q = owned(info, lax.rem(info[1] + d, X))
            out[...] = total[pl.ds(pl.multiple_of(q * 128, 128), 128), :].astype(BF16)

    @pl.when(info[0] == 0)
    def _():
        for out in (o0, o1, o2, o3):
            out[...] = jnp.zeros_like(out)


def late_integrals(info, own, following):
    rows, aux = own.shape
    return pl.pallas_call(
        late_integrals_kernel,
        in_specs=[SMEM, ANY, ANY],
        out_specs=[VMEM] * 4,
        out_shape=[jax.ShapeDtypeStruct((Q, rows), BF16)] * 4,
        scratch_shapes=[
            pltpu.VMEM((rows, aux), BF16),
            pltpu.VMEM((rows, aux), BF16),
            pltpu.VMEM((rows, rows), F32),
            pltpu.SemaphoreType.DMA((CHUNKS,)),
            pltpu.SemaphoreType.DMA((CHUNKS,)),
        ],
        compiler_params=params(40),
        cost_estimate=pl.CostEstimate(flops=0, bytes_accessed=0, transcendentals=0),
        name="late_integrals",
    )(info, own, following)


def block_transposed(wide):
    turned = wide.T
    top, bottom = turned[:64], turned[64:]
    low = lax.broadcasted_iota(jnp.int32, (64, 128), 1) < 64
    first = jnp.where(low, top, pltpu.roll(bottom, 64, 1))
    second = jnp.where(low, pltpu.roll(top, 64, 1), bottom)
    return jnp.concatenate([first, second], axis=0), turned


def diagonal_blocks(square):
    return square[:64, :64] + pltpu.roll(square[64:, :], 64, 1)[:, :64]


def tilde_rows(integrals, q, left, right, virt, keep, store):
    first = jnp.zeros((128, 128), F32)
    second = jnp.zeros((128, 128), F32)
    upper = lax.broadcasted_iota(jnp.int32, (128, 1), 0) < 64
    lower = lax.broadcasted_iota(jnp.int32, (1, 128), 1) < 64
    along = jnp.concatenate([virt, virt], axis=1).astype(F32)
    down = jnp.broadcast_to(along, (128, 128)).T
    gap_left = jnp.where(upper, left(2 * q), left(2 * q + 1)) - down
    for J in range(4):
        at = slice(J * 128, (J + 1) * 128)
        gap_right = jnp.where(lower, right(2 * J), right(2 * J + 1)) - along
        amp = (keep * integrals(at) / (gap_left + gap_right)).astype(BF16)
        wide = amp.astype(F32)
        swapped, turned = block_transposed(wide)
        tilde_wide = (2.0 * wide - swapped).astype(BF16).astype(F32)
        tilde = tilde_wide.astype(BF16)
        tilde_turned = tilde_wide.T.astype(BF16)
        first += rows_product(tilde, amp)
        second += rows_product(tilde_turned, turned.astype(BF16))
        store(J, tilde, tilde_turned)
    return diagonal_blocks(first), diagonal_blocks(second)


def early_tilde_kernel(
    info, kept, own_energy, inner_energy, here, there, inner_mine, inner_other, virt, out, density
):
    q = owned(info, info[1])
    left_home = info[0] == 0

    def own(i):
        return own_energy[i]

    def left(i):
        return jnp.where(left_home, own_energy[i], inner_energy[i])

    def right(j):
        return jnp.where(left_home, inner_energy[j], own_energy[j])

    def store_own(J, tilde, turned):
        out[J] = tilde

    own_first, _ = tilde_rows(
        lambda at: here[0:128, at].astype(F32) + there[0:128, at].astype(F32), q, own, own, virt[...], 1.0, store_own
    )

    def inner(at):
        mine, theirs = inner_mine[:, at], inner_other[:, at]
        return jnp.concatenate(
            [jnp.where(left_home, mine, theirs), jnp.where(left_home, theirs, mine)], axis=0
        )

    def store_inner(J, tilde, turned):
        out[4 + J] = jnp.where(left_home, tilde, turned)

    first, second = tilde_rows(
        inner, q, left, right, virt[...], kept[info[3] - info[0]].astype(F32), store_inner
    )
    density[...] = own_first + jnp.where(left_home, first + second, 0.0)


def early_tilde(*operands):
    return pl.pallas_call(
        early_tilde_kernel,
        in_specs=[SMEM] * 4 + [VMEM] * 5,
        out_specs=[VMEM, VMEM],
        out_shape=[jax.ShapeDtypeStruct((8, 128, 128), BF16), jax.ShapeDtypeStruct((64, 64), F32)],
        compiler_params=pltpu.CompilerParams(vmem_limit_bytes=32 * MIB),
        cost_estimate=pl.CostEstimate(flops=0, bytes_accessed=0, transcendentals=0),
        name="early_tilde",
    )(*operands)


def late_tilde_kernel(
    info, kept, left_energy, right_energy, mine, partner, early, virt, straight, turned, density
):
    def outer(at):
        return mine[:, at].astype(F32) + partner[:, at].astype(F32)

    def left(i):
        return left_energy[i]

    def right(j):
        return right_energy[j]

    def store(J, tilde, tilde_turned):
        straight[J * 128 : (J + 1) * 128, :] = tilde
        turned[J * 128 : (J + 1) * 128, :] = tilde_turned

    first, second = tilde_rows(
        outer, owned(info, info[1]), left, right, virt[...], kept[info[3] - info[0] + 1].astype(F32), store
    )
    density[...] = early[...] + jnp.where(info[0] == 0, first + second, 0.0)


def late_tilde(*operands):
    return pl.pallas_call(
        late_tilde_kernel,
        in_specs=[SMEM] * 4 + [VMEM] * 4,
        out_specs=[VMEM] * 3,
        out_shape=[
            jax.ShapeDtypeStruct((512, 128), BF16),
            jax.ShapeDtypeStruct((512, 128), BF16),
            jax.ShapeDtypeStruct((64, 64), F32),
        ],
        compiler_params=params(32),
        cost_estimate=pl.CostEstimate(flops=0, bytes_accessed=0, transcendentals=0),
        name="late_tilde",
    )(*operands)


def gamma_kernel(
    info, e0, e1, e2, e3, p0, p1, p2, p3, own, other, following, preceding, out,
    slab, result, factors, sem_own, sem_other, sem_outer, sem_out,
):
    rows = own.shape[0]
    left_home = info[0] == 1
    own_copies = fetched(own, slab.at[:rows], sem_own)
    other_copies = fetched(other, slab.at[rows : 2 * rows], sem_other)
    left_copies = fetched(following, slab.at[2 * rows :], sem_outer)
    right_copies = fetched(preceding, slab.at[2 * rows :], sem_outer)
    for c in range(CHUNKS):
        own_copies[c].start()
        other_copies[c].start()

        @pl.when(left_home)
        def _():
            left_copies[c].start()

        @pl.when(jnp.logical_not(left_home))
        def _():
            right_copies[c].start()

    for d, (early, late) in enumerate(((e0, p0), (e1, p1), (e2, p2), (e3, p3))):
        q = owned(info, lax.rem(info[1] + X - d, X))
        here = pl.ds(pl.multiple_of(q * 128, 128), 128)
        for J in range(4):
            factors[here, J * 128 : (J + 1) * 128] = early[J]

        q_late = owned_late(info, lax.rem(info[1] + X - d, X))
        here_late = pl.ds(pl.multiple_of(q_late * 128, 128), 128)

        @pl.when(jnp.logical_not(left_home))
        def _():
            column = pl.ds(pl.multiple_of(2 * rows + q_late * 128, 128), 128)
            for J in range(4):
                factors[here, rows + J * 128 : rows + (J + 1) * 128] = early[4 + J]
                factors[J * 128 : (J + 1) * 128, column] = late[J * 128 : (J + 1) * 128]

        @pl.when(left_home)
        def _():
            column = pl.ds(pl.multiple_of(rows + q * 128, 128), 128)
            for J in range(4):
                factors[J * 128 : (J + 1) * 128, column] = early[4 + J]
                factors[here_late, 2 * rows + J * 128 : 2 * rows + (J + 1) * 128] = late[
                    J * 128 : (J + 1) * 128
                ]

    written = fetched(result, out, sem_out)
    for c, at in enumerate(chunks(own.shape[1])):
        own_copies[c].wait()
        other_copies[c].wait()

        @pl.when(left_home)
        def _():
            left_copies[c].wait()

        @pl.when(jnp.logical_not(left_home))
        def _():
            right_copies[c].wait()

        result[:, at] = product(factors[...], slab[:, at]).astype(BF16)
        written[c].start()
    for copy in written:
        copy.wait()


def gamma_block(info, early, late, own, other, following, preceding):
    rows, aux = own.shape
    return pl.pallas_call(
        gamma_kernel,
        in_specs=[SMEM] + [VMEM] * 8 + [ANY] * 4,
        out_specs=ANY,
        out_shape=jax.ShapeDtypeStruct((rows, aux), BF16),
        scratch_shapes=[
            pltpu.VMEM((3 * rows, aux), BF16),
            pltpu.VMEM((rows, aux), BF16),
            pltpu.VMEM((rows, 3 * rows), BF16),
            *[pltpu.SemaphoreType.DMA((CHUNKS,))] * 4,
        ],
        compiler_params=params(56),
        cost_estimate=pl.CostEstimate(flops=0, bytes_accessed=0, transcendentals=0),
        name="gamma_block",
    )(info, *early, *late, own, other, following, preceding)


def along_x(value, by):
    return lax.ppermute(
        value, "aux", [(a, a // X * X + (a + by) % X) for a in range(lax.axis_size("aux"))]
    )


def across_y(value):
    return lax.ppermute(value, "aux", [(a, a ^ X ^ 1) for a in range(lax.axis_size("aux"))])


def from_cores(core, value, occ_to, aux_to=lambda a: a):
    aux, occ = lax.axis_size("aux"), lax.axis_size("occ")
    return lax.ppermute(
        value,
        ("aux", "occ"),
        [
            (a * occ + k, aux_to(a) * occ + occ_to(k) % occ)
            for a in range(aux)
            for k in range(core, occ, 2)
        ],
    )


def swapped(value, axis, other):
    return lax.ppermute(value, axis, [(k, other(k)) for k in range(lax.axis_size(axis))])


def together(values):
    return lax.optimization_barrier(tuple(values))


def after(value, *earlier):
    return lax.optimization_barrier((value, *earlier))[0]


def body(orbital_slabs, occ_energy, virt_energy, pair_kept):
    occ_count, virt_count, aux_count = orbital_slabs.shape
    rows = occ_count * virt_count
    occ = lax.axis_size("occ")
    slabs = orbital_slabs.reshape(rows, aux_count)
    place = lax.axis_index("occ")
    core = lax.rem(place, 2)
    aux_place = lax.axis_index("aux")
    x = lax.rem(aux_place, X)
    info = jnp.stack([core, x, aux_place // X, place]).astype(jnp.int32)
    energy = occ_energy.astype(F32)

    following = lax.ppermute(slabs, "occ", [(k, (k - 1) % occ) for k in range(0, occ, 2)])
    other = swapped(slabs, "occ", lambda k: k ^ 1)
    inner_energy = swapped(energy, "occ", lambda k: k ^ 1)
    outer_energy = from_cores(1, inner_energy, lambda k: k - 3, lambda a: a ^ 1)
    virt = virt_energy.reshape(1, virt_count)

    pieces = early_integrals(info, slabs, other)
    arrived = together(along_x(pieces[d], d) for d in (1, 2, 3))
    sums = pieces[0].astype(F32)
    for value in arrived:
        sums = sums + value.astype(F32)
    scattered = sums.astype(BF16)
    there, outer_energy = together([across_y(scattered), outer_energy])
    inner = scattered[Q:].astype(F32) + there[Q:].astype(F32)
    inner_other = swapped(inner, "occ", lambda k: k ^ 1)
    tilde, density = early_tilde(
        info, pair_kept, energy, inner_energy, scattered, there, inner, inner_other, virt
    )
    own_tilde = tilde

    following = after(following, tilde)
    pieces = late_integrals(info, slabs, following)
    preceding = lax.ppermute(
        after(slabs, pieces[0]), "occ", [(k, (k + 1) % occ) for k in range(1, occ, 2)]
    )
    arrived = together(
        from_cores(1, pieces[d], lambda k: k - 1, lambda a, d=d: a // X * X + (a + d) % X)
        for d in range(X)
    )
    sums = arrived[0].astype(F32)
    for value in arrived[1:]:
        sums = sums + value.astype(F32)
    sums = sums.astype(BF16)
    partner = from_cores(0, sums, lambda k: k, lambda a: a ^ X ^ 1)
    straight, turned, density = late_tilde(
        info, pair_kept, inner_energy, outer_energy, sums, partner, density, virt
    )
    left = from_cores(0, straight, lambda k: k + 1)
    right = from_cores(0, turned, lambda k: k + 2, lambda a: a ^ 1)

    tilde = jnp.where(core == 1, left, right)
    own_tilde = after(own_tilde, left)
    early = [own_tilde, *together(along_x(own_tilde, d) for d in (1, 2, 3))]
    late = [tilde, *together(along_x(tilde, d) for d in (1, 2, 3))]
    gamma = gamma_block(info, early, late, slabs, other, following, preceding)

    for flip, earlier in ((4, ()), (8, (left,)), (16, (early[1],)), (2, (preceding, tilde))):
        density = after(density, *earlier)
        density = density + swapped(density, "occ", lambda k, flip=flip: k ^ flip)
    parts = [along_x(density, d) for d in range(1, X)]
    gamma, density, *parts = together([gamma, density, *parts])
    density = (density + parts[1]) + (parts[0] + parts[2])
    density = density + swapped(density, "occ", lambda k: k ^ 1)
    virt_density = density / (4.0 * occ_count * occ_count * virt_count)
    return gamma.reshape(occ_count, virt_count, aux_count), virt_density


def solution(mesh):
    return jax.shard_map(
        body,
        mesh=mesh,
        in_specs=(P("occ", None, "aux"), P("occ"), P(), P()),
        out_specs=(P("occ", None, "aux"), P()),
        check_vma=False,
    )
```
